768 devices in a mesh: row: 96 (over y_lo, z, x), col: 8 (over y_hi, core).
Axes of the slice: x: 4, y: 8 (y_hi: 4, y_lo: 2; y = y_hi * 2 + y_lo), z: 12, core: 2. Of those that a mesh axis runs over, the one named last changes fastest.
Arguments:
- momentum: bfloat16 [24576, 3072], P('row', 'col'), may hold values from -0.125 to 0.125
Outputs:
- update: bfloat16 [24576, 3072], P('row', 'col')
The draws below stay inside these ranges and needn't reach their ends.
All inputs are finite; a program needn't handle non-finite values.
Results may differ from the reference program's by a relative error of at most 0.0084.
Values may be sent and summed in bfloat16 or wider, within the bound.
No kernel may reach another device: no remote copies, remote signals or barrier semaphores. Data moves between devices by JAX's collectives and lax.ppermute only.
A program may use at most 32 MiB of HBM per device.

```python
import math
import jax
import jax.numpy as jnp

F = 24576
D = 3072


def raised(entries, rng, source, target, parts, factor):
    def block_of(position):
        return (jnp.arange(entries.shape[position]) // (entries.shape[position] // parts)).reshape((-1,) + (1,) * (entries.ndim - 1 - position))

    near = jax.random.permutation(rng, parts)[block_of(target)]
    far = (block_of(target) + parts // 2) % parts
    return jnp.where((block_of(source) == near) | (block_of(source) == far), factor * entries, entries)


def level_of(own_key, dims, shards, smallest, largest):
    level = 1.0
    for axis_at, blocks in shards:
        draws = jax.random.uniform(jax.random.fold_in(jax.random.fold_in(own_key, 6), axis_at), (blocks,), jnp.float32, smallest / len(shards), largest / len(shards))
        level = level * jnp.repeat(jnp.exp(draws), dims[axis_at] // blocks).reshape((-1,) + (1,) * (len(dims) - 1 - axis_at))
    return level


def gaussian_with(key, dims, spread, reach, pieces, heavy, dtype=jnp.bfloat16):
    values = spread * jax.random.normal(key, dims, jnp.float32)
    if pieces:
        values = values * level_of(key, dims, pieces, -0.22, 0.18)
    return jnp.clip(raised(values, jax.random.fold_in(key, 3), *heavy), -reach, reach).astype(dtype)


def setup_inputs(seed: int = 0) -> dict:
    streams_of = jax.random.split(jax.random.key(seed), 2)
    return {
        "momentum": gaussian_with(streams_of[0], (F, D), F ** -0.5, 0.125, ((0, 96), (1, 8)), (0, 1, 96, 4.75)),
    }


coef_first = 3.4445
coef_middle = -4.775
coef_last = 2.0315

def reference(momentum):
    gram = jnp.dot(momentum.T, momentum, preferred_element_type=jnp.float32).astype(jnp.bfloat16)
    mixed = jnp.dot(momentum, gram, preferred_element_type=jnp.float32).astype(jnp.bfloat16)
    second = jnp.dot(mixed, gram, preferred_element_type=jnp.float32)
    rms_scale = 0.2 * math.sqrt(max(F, D))
    total = coef_first * momentum.astype(jnp.float32) + coef_middle * mixed.astype(jnp.float32) + coef_last * second
    return (rms_scale * total).astype(jnp.bfloat16)
```

```python
import math

import jax
import jax.numpy as jnp
from jax import lax
from jax.sharding import Mesh
from jax.sharding import PartitionSpec as P

coef_first = 3.4445
coef_middle = -4.775
coef_last = 2.0315

axes = ("yl", "z", "x", "yh", "core")
row_axes = ("yl", "z", "x")
col_axes = ("yh", "core")
axis_sizes = (2, 12, 4, 4, 2)


def spread(block, names, count):
    copies = jnp.broadcast_to(block[None], (count,) + block.shape)
    return lax.all_to_all(copies, names, 0, 0, tiled=True)


def gather_columns(block):
    near = spread(block, "yh", 4)
    far = lax.ppermute(near, "core", [(0, 1), (1, 0)])
    return jnp.concatenate([near, far], axis=0)


def body(momentum):
    with jax.named_scope("panel"):
        panel = gather_columns(momentum)
    with jax.named_scope("gram"):
        partial = lax.dot_general(
            panel, momentum, (((1,), (0,)), ((), ())), preferred_element_type=jnp.float32
        ).astype(jnp.bfloat16)
    with jax.named_scope("reduce"):
        parts = lax.all_to_all(partial, ("yl", "x"), 0, 0, tiled=True)
        block = jnp.sum(parts.astype(jnp.float32), axis=0).astype(jnp.bfloat16)
        parts = lax.all_to_all(block.reshape(12, 32, 384), "z", 0, 0, tiled=True)
        piece = jnp.sum(parts.astype(jnp.float32), axis=0).astype(jnp.bfloat16)
    with jax.named_scope("collect"):
        block = spread(piece, "z", 12).reshape(384, 384)
        gram = spread(block, ("yl", "x"), 8)

    def times_gram(left):
        return lax.dot_general(
            left, gram, (((0, 2), (0, 1)), ((), ())), preferred_element_type=jnp.float32
        )

    with jax.named_scope("mixed"):
        mixed = times_gram(panel).astype(jnp.bfloat16)
    with jax.named_scope("mixed_panel"):
        mixed_panel = gather_columns(mixed)
    with jax.named_scope("second"):
        second = times_gram(mixed_panel)
        rms_scale = 0.2 * math.sqrt(max(momentum.shape[0] * 96, 3072))
        total = (
            coef_first * momentum.astype(jnp.float32)
            + coef_middle * mixed.astype(jnp.float32)
            + coef_last * second
        )
        return (rms_scale * total).astype(jnp.bfloat16)


def solution(mesh):
    fine = Mesh(mesh.devices.reshape(axis_sizes), axes)
    return jax.shard_map(
        body,
        mesh=fine,
        in_specs=(P(row_axes, col_axes),),
        out_specs=P(row_axes, col_axes),
        check_vma=False,
    )
```

```python
import math

import jax
import jax.numpy as jnp
from jax import lax
from jax.sharding import Mesh
from jax.sharding import PartitionSpec as P

coef_first = 3.4445
coef_middle = -4.775
coef_last = 2.0315

axes = ("yl", "z", "x", "yh", "core")
row_axes = ("yl", "z", "x")
col_axes = ("yh", "core")
axis_sizes = (2, 12, 4, 4, 2)
chunks = ((0, 384),)


def exchange(blocks, names):
    return lax.all_to_all(blocks, names, 0, 0, tiled=True)


def spread(block, names, count):
    return exchange(jnp.broadcast_to(block[None], (count,) + block.shape), names)


def add_up(parts):
    return jnp.sum(parts.astype(jnp.float32), axis=0).astype(jnp.bfloat16)


def gather_columns(block):
    near = lax.all_gather(block, "yh", axis=0)
    far = lax.ppermute(near, "core", [(0, 1), (1, 0)])
    return jnp.concatenate([near, far], axis=0)


def times(left, right):
    return lax.dot_general(
        left, right, (((0, 2), (0, 1)), ((), ())), preferred_element_type=jnp.float32
    )


def body(momentum):
    with jax.named_scope("panel"):
        panel = gather_columns(momentum)
    grams = []
    for start, stop in chunks:
        width = stop - start
        with jax.named_scope("gram"):
            partial = lax.dot_general(
                panel,
                momentum[:, start:stop],
                (((1,), (0,)), ((), ())),
                preferred_element_type=jnp.float32,
            ).astype(jnp.bfloat16)
        with jax.named_scope("reduce"):
            block = add_up(exchange(partial, ("yl", "x")))
            piece = add_up(exchange(block.reshape(12, 32, width), "z"))
        with jax.named_scope("collect"):
            block = spread(piece, "z", 12).reshape(384, width)
            grams.append(spread(block, ("yl", "x"), 8))
    with jax.named_scope("mixed"):
        mixed = [times(panel, gram).astype(jnp.bfloat16) for gram in grams]
    with jax.named_scope("mixed_panel"):
        mixed_panels = [gather_columns(part) for part in mixed]
    with jax.named_scope("second"):
        gram = jnp.concatenate(grams, axis=2)
        second = sum(
            times(part, gram[:, start:stop])
            for part, (start, stop) in zip(mixed_panels, chunks)
        )
        rms_scale = 0.2 * math.sqrt(max(momentum.shape[0] * 96, 3072))
        total = (
            coef_first * momentum.astype(jnp.float32)
            + coef_middle * jnp.concatenate(mixed, axis=1).astype(jnp.float32)
            + coef_last * second
        )
        return (rms_scale * total).astype(jnp.bfloat16)


def solution(mesh):
    fine = Mesh(mesh.devices.reshape(axis_sizes), axes)
    return jax.shard_map(
        body,
        mesh=fine,
        in_specs=(P(row_axes, col_axes),),
        out_specs=P(row_axes, col_axes),
        check_vma=False,
    )
```

```python
import math

import jax
import jax.numpy as jnp
import numpy as np
from jax import lax
from jax.sharding import Mesh
from jax.sharding import PartitionSpec as P

coef_first = 3.4445
coef_middle = -4.775
coef_last = 2.0315

axes = ("yl", "z", "x", "yh", "core")
row_axes = ("yl", "z", "x")
col_axes = ("yh", "core")
axis_sizes = (2, 12, 4, 4, 2)


def grouped(key, place):
    members = {}
    for device, at in enumerate(np.ndindex(*axis_sizes)):
        members.setdefault(key(*at), []).append((place(*at), device))
    return [[device for _, device in sorted(group)] for group in members.values()]


def along_x(core):
    return grouped(
        lambda yl, z, x, yh, c: (yl, z, -1, yh, c) if c == core else (-1, z // 2, x, yh, c),
        lambda yl, z, x, yh, c: x if c == core else 2 * yl + z % 2,
    )


stages = (
    (4, along_x(0)),
    (4, along_x(1)),
    (6, grouped(lambda yl, z, x, yh, c: (yl, z % 2, x, yh, c), lambda yl, z, x, yh, c: z)),
)


def exchange(blocks, groups):
    return lax.all_to_all(blocks, axes, 0, 0, axis_index_groups=groups, tiled=True)


def add_up(parts):
    return jnp.sum(parts.astype(jnp.float32), axis=0).astype(jnp.bfloat16)


def gather_columns(block):
    near = lax.all_gather(block, "yh", axis=0)
    far = lax.ppermute(near, "core", [(0, 1), (1, 0)])
    return jnp.concatenate([near, far], axis=0)


def times(left, right):
    return lax.dot_general(
        left, right, (((0, 2), (0, 1)), ((), ())), preferred_element_type=jnp.float32
    )


def body(momentum):
    with jax.named_scope("panel"):
        panel = gather_columns(momentum)
    with jax.named_scope("gram"):
        piece = lax.dot_general(
            panel, momentum, (((1,), (0,)), ((), ())), preferred_element_type=jnp.float32
        ).astype(jnp.bfloat16)
    width = momentum.shape[1]
    with jax.named_scope("reduce"):
        for count, groups in stages:
            piece = add_up(exchange(piece.reshape(count, -1, width), groups))
    with jax.named_scope("collect"):
        for count, groups in reversed(stages):
            piece = piece.reshape(-1, width)
            piece = exchange(jnp.broadcast_to(piece[None], (count,) + piece.shape), groups)
        gram = piece.reshape(8, width, width)
    with jax.named_scope("mixed"):
        mixed = times(panel, gram).astype(jnp.bfloat16)
    with jax.named_scope("mixed_panel"):
        mixed_panel = gather_columns(mixed)
    with jax.named_scope("second"):
        second = times(mixed_panel, gram)
        rms_scale = 0.2 * math.sqrt(max(momentum.shape[0] * 96, 3072))
        total = (
            coef_first * momentum.astype(jnp.float32)
            + coef_middle * mixed.astype(jnp.float32)
            + coef_last * second
        )
        return (rms_scale * total).astype(jnp.bfloat16)


def solution(mesh):
    fine = Mesh(mesh.devices.reshape(axis_sizes), axes)
    return jax.shard_map(
        body,
        mesh=fine,
        in_specs=(P(row_axes, col_axes),),
        out_specs=P(row_axes, col_axes),
        check_vma=False,
    )
```

```python
import math

import jax
import jax.numpy as jnp
import numpy as np
from jax import lax
from jax.sharding import Mesh
from jax.sharding import PartitionSpec as P

coef_first = 3.4445
coef_middle = -4.775
coef_last = 2.0315

axes = ("yl", "z", "x", "yh", "core")
row_axes = ("yl", "z", "x")
col_axes = ("yh", "core")
axis_sizes = (2, 12, 4, 4, 2)


def grouped(key, place):
    members = {}
    for device, at in enumerate(np.ndindex(*axis_sizes)):
        members.setdefault(key(*at), []).append((place(*at), device))
    return [[device for _, device in sorted(group)] for group in members.values()]


def along_x(core):
    return grouped(
        lambda yl, z, x, yh, c: (yl, z, -1, yh, c) if c == core else (-1, z // 2, x, yh, c),
        lambda yl, z, x, yh, c: x if c == core else 2 * yl + z % 2,
    )


stages = (
    (4, along_x(0)),
    (4, along_x(1)),
    (6, grouped(lambda yl, z, x, yh, c: (yl, z % 2, x, yh, c), lambda yl, z, x, yh, c: z)),
)


wide = grouped(
    lambda yl, z, x, yh, c: (-1, z // 2, -1, yh, c),
    lambda yl, z, x, yh, c: 4 * x + 2 * yl + z % 2 if c == 0 else 4 * (2 * yl + z % 2) + x,
)


def exchange(blocks, groups):
    return lax.all_to_all(blocks, axes, 0, 0, axis_index_groups=groups, tiled=True)


def add_up(parts):
    return sum(parts[i].astype(jnp.float32) for i in range(parts.shape[0])).astype(jnp.bfloat16)


def gather_columns(block):
    near = lax.all_gather(block, "yh", axis=0)
    far = lax.ppermute(near, "core", [(0, 1), (1, 0)])
    return jnp.concatenate([near, far], axis=0)


def times(left, right):
    return lax.dot_general(
        left, right, (((0, 2), (0, 1)), ((), ())), preferred_element_type=jnp.float32
    )


def body(momentum):
    with jax.named_scope("panel"):
        panel = gather_columns(momentum)
    with jax.named_scope("gram"):
        piece = lax.dot_general(
            panel, momentum, (((1,), (0,)), ((), ())), preferred_element_type=jnp.float32
        ).astype(jnp.bfloat16)
    width = momentum.shape[1]
    with jax.named_scope("reduce"):
        for count, groups in stages:
            piece = add_up(exchange(piece.reshape(count, -1, width), groups))
    with jax.named_scope("collect"):
        for count, groups in (stages[2], (16, wide)):
            piece = piece.reshape(-1, width)
            piece = exchange(jnp.broadcast_to(piece[None], (count,) + piece.shape), groups)
        gram = piece.reshape(8, width, width)
    with jax.named_scope("mixed"):
        mixed = times(panel, gram).astype(jnp.bfloat16)
    with jax.named_scope("mixed_panel"):
        mixed_panel = gather_columns(mixed)
    with jax.named_scope("second"):
        second = times(mixed_panel, gram)
        rms_scale = 0.2 * math.sqrt(max(momentum.shape[0] * 96, 3072))
        total = (
            coef_first * momentum.astype(jnp.float32)
            + coef_middle * mixed.astype(jnp.float32)
            + coef_last * second
        )
        return (rms_scale * total).astype(jnp.bfloat16)


def solution(mesh):
    fine = Mesh(mesh.devices.reshape(axis_sizes), axes)
    return jax.shard_map(
        body,
        mesh=fine,
        in_specs=(P(row_axes, col_axes),),
        out_specs=P(row_axes, col_axes),
        check_vma=False,
    )
```

```python
import math

import jax
import jax.numpy as jnp
import numpy as np
from jax import lax
from jax.sharding import Mesh
from jax.sharding import PartitionSpec as P

coef_first = 3.4445
coef_middle = -4.775
coef_last = 2.0315

axes = ("yl", "z", "x", "yh", "core")
row_axes = ("yl", "z", "x")
col_axes = ("yh", "core")
axis_sizes = (2, 12, 4, 4, 2)
around = (0, 2, 1, 3)


def grouped(key, place):
    members = {}
    for device, at in enumerate(np.ndindex(*axis_sizes)):
        members.setdefault(key(*at), []).append((place(*at), device))
    return [[device for _, device in sorted(group)] for group in members.values()]


def along_x(core):
    return grouped(
        lambda yl, z, x, yh, c: (yl, z, -1, yh, c) if c == core else (-1, z // 2, x, yh, c),
        lambda yl, z, x, yh, c: around[x] if c == core else 2 * yl + z % 2,
    )


stages = (
    (4, along_x(1)),
    (4, along_x(0)),
    (6, grouped(lambda yl, z, x, yh, c: (yl, z % 2, x, yh, c), lambda yl, z, x, yh, c: z)),
)


wide = grouped(
    lambda yl, z, x, yh, c: (-1, z // 2, -1, yh, c),
    lambda yl, z, x, yh, c: 4 * around[x] + 2 * yl + z % 2 if c == 1 else 4 * (2 * yl + z % 2) + around[x],
)


def exchange(blocks, groups):
    return lax.all_to_all(blocks, axes, 0, 0, axis_index_groups=groups, tiled=True)


def add_up(parts):
    return sum(parts[i].astype(jnp.float32) for i in range(parts.shape[0])).astype(jnp.bfloat16)


def gather_columns(block):
    near = lax.all_gather(block, "yh", axis=0)
    far = lax.ppermute(near, "core", [(0, 1), (1, 0)])
    return near, far


def times(left, right):
    return lax.dot_general(
        left, right, (((0, 2), (0, 1)), ((), ())), preferred_element_type=jnp.float32
    )


def body(momentum):
    with jax.named_scope("panel"):
        panel = jnp.concatenate(gather_columns(momentum), axis=0)
    with jax.named_scope("gram"):
        piece = lax.dot_general(
            panel, momentum, (((1,), (0,)), ((), ())), preferred_element_type=jnp.float32
        ).astype(jnp.bfloat16)
    width = momentum.shape[1]
    with jax.named_scope("reduce"):
        for count, groups in stages:
            piece = add_up(exchange(piece.reshape(count, -1, width), groups))
    with jax.named_scope("collect"):
        for count, groups in (stages[2], (16, wide)):
            piece = piece.reshape(-1, width)
            piece = exchange(jnp.broadcast_to(piece[None], (count,) + piece.shape), groups)
        gram = piece.reshape(8, width, width)
    with jax.named_scope("mixed"):
        mixed = times(panel, gram).astype(jnp.bfloat16)
    with jax.named_scope("mixed_panel"):
        near, far = gather_columns(mixed)
    with jax.named_scope("second"):
        second = times(near, gram[:4]) + times(far, gram[4:])
        rms_scale = 0.2 * math.sqrt(max(momentum.shape[0] * 96, 3072))
        total = (
            coef_first * momentum.astype(jnp.float32)
            + coef_middle * mixed.astype(jnp.float32)
            + coef_last * second
        )
        return (rms_scale * total).astype(jnp.bfloat16)


def solution(mesh):
    fine = Mesh(mesh.devices.reshape(axis_sizes), axes)
    return jax.shard_map(
        body,
        mesh=fine,
        in_specs=(P(row_axes, col_axes),),
        out_specs=P(row_axes, col_axes),
        check_vma=False,
    )
```

```python
import math

import jax
import jax.numpy as jnp
import numpy as np
from jax import lax
from jax.sharding import Mesh
from jax.sharding import PartitionSpec as P

coef_first = 3.4445
coef_middle = -4.775
coef_last = 2.0315

axes = ("yl", "z", "x", "yh", "core")
row_axes = ("yl", "z", "x")
col_axes = ("yh", "core")
axis_sizes = (2, 12, 4, 4, 2)
around = (0, 1, 3, 2)


def grouped(key, place):
    members = {}
    for device, at in enumerate(np.ndindex(*axis_sizes)):
        members.setdefault(key(*at), []).append((place(*at), device))
    return [[device for _, device in sorted(group)] for group in members.values()]


def along_x(core):
    return grouped(
        lambda yl, z, x, yh, c: (yl, z, -1, yh, c) if c == core else (-1, z // 2, x, yh, c),
        lambda yl, z, x, yh, c: around[x] if c == core else 2 * yl + z % 2,
    )


stages = (
    (4, along_x(1)),
    (4, along_x(0)),
    (6, grouped(lambda yl, z, x, yh, c: (yl, z % 2, x, yh, c), lambda yl, z, x, yh, c: z)),
)


wide = grouped(
    lambda yl, z, x, yh, c: (-1, z // 2, -1, yh, c),
    lambda yl, z, x, yh, c: 4 * around[x] + 2 * yl + z % 2 if c == 1 else 4 * (2 * yl + z % 2) + around[x],
)


def exchange(blocks, groups):
    return lax.all_to_all(blocks, axes, 0, 0, axis_index_groups=groups, tiled=True)


def add_up(parts):
    return sum(parts[i].astype(jnp.float32) for i in range(parts.shape[0])).astype(jnp.bfloat16)


def gather_columns(block):
    near = lax.all_gather(block, "yh", axis=0)
    far = lax.ppermute(near, "core", [(0, 1), (1, 0)])
    return near, far


def times(left, right):
    return lax.dot_general(
        left, right, (((0, 2), (0, 1)), ((), ())), preferred_element_type=jnp.float32
    )


def body(momentum):
    with jax.named_scope("panel"):
        panel = jnp.concatenate(gather_columns(momentum), axis=0)
    with jax.named_scope("gram"):
        piece = lax.dot_general(
            panel, momentum, (((1,), (0,)), ((), ())), preferred_element_type=jnp.float32
        ).astype(jnp.bfloat16)
    width = momentum.shape[1]
    with jax.named_scope("reduce"):
        for count, groups in stages:
            piece = add_up(exchange(piece.reshape(count, -1, width), groups))
    with jax.named_scope("collect"):
        for count, groups in (stages[2], (16, wide)):
            piece = piece.reshape(-1, width)
            piece = exchange(jnp.broadcast_to(piece[None], (count,) + piece.shape), groups)
        gram = piece.reshape(8, width, width)
    with jax.named_scope("mixed"):
        mixed = times(panel, gram).astype(jnp.bfloat16)
    with jax.named_scope("mixed_panel"):
        near, far = gather_columns(mixed)
    with jax.named_scope("second"):
        rms_scale = 0.2 * math.sqrt(max(momentum.shape[0] * 96, 3072))
        started = (
            coef_first * momentum.astype(jnp.float32)
            + coef_middle * mixed.astype(jnp.float32)
            + coef_last * times(near, gram[:4])
        )
        total = started + coef_last * times(far, gram[4:])
        return (rms_scale * total).astype(jnp.bfloat16)


def solution(mesh):
    fine = Mesh(mesh.devices.reshape(axis_sizes), axes)
    return jax.shard_map(
        body,
        mesh=fine,
        in_specs=(P(row_axes, col_axes),),
        out_specs=P(row_axes, col_axes),
        check_vma=False,
    )
```

```python
import math

import jax
import jax.numpy as jnp
import numpy as np
from jax import lax
from jax.sharding import Mesh
from jax.sharding import PartitionSpec as P

coef_first = 3.4445
coef_middle = -4.775
coef_last = 2.0315

axes = ("yl", "z", "x", "yh", "core")
row_axes = ("yl", "z", "x")
col_axes = ("yh", "core")
axis_sizes = (2, 12, 4, 4, 2)
around = ((0, 1, 3, 2), (0, 2, 3, 1))


def grouped(key, place):
    members = {}
    for device, at in enumerate(np.ndindex(*axis_sizes)):
        members.setdefault(key(*at), []).append((place(*at), device))
    return [[device for _, device in sorted(group)] for group in members.values()]


def along_x(core):
    return grouped(
        lambda yl, z, x, yh, c: (yl, z, -1, yh, c) if c == core else (-1, z // 2, x, yh, c),
        lambda yl, z, x, yh, c: around[c][x] if c == core else 2 * yl + z % 2,
    )


stages = (
    (4, along_x(1)),
    (4, along_x(0)),
    (6, grouped(lambda yl, z, x, yh, c: (yl, z % 2, x, yh, c), lambda yl, z, x, yh, c: z)),
)


wide = grouped(
    lambda yl, z, x, yh, c: (-1, z // 2, -1, yh, c),
    lambda yl, z, x, yh, c: 4 * around[c][x] + 2 * yl + z % 2 if c == 1 else 4 * (2 * yl + z % 2) + around[c][x],
)


def exchange(blocks, groups):
    return lax.all_to_all(blocks, axes, 0, 0, axis_index_groups=groups, tiled=True)


def add_up(parts):
    return sum(parts[i].astype(jnp.float32) for i in range(parts.shape[0])).astype(jnp.bfloat16)


def gather_columns(block):
    near = lax.all_gather(block, "yh", axis=0)
    far = lax.ppermute(near, "core", [(0, 1), (1, 0)])
    return near, far


def times(left, right):
    return lax.dot_general(
        left, right, (((0, 2), (0, 1)), ((), ())), preferred_element_type=jnp.float32
    )


def body(momentum):
    with jax.named_scope("panel"):
        panel = jnp.concatenate(gather_columns(momentum), axis=0)
    with jax.named_scope("gram"):
        piece = lax.dot_general(
            panel, momentum, (((1,), (0,)), ((), ())), preferred_element_type=jnp.float32
        ).astype(jnp.bfloat16)
    width = momentum.shape[1]
    with jax.named_scope("reduce"):
        for count, groups in stages:
            piece = add_up(exchange(piece.reshape(count, -1, width), groups))
    with jax.named_scope("collect"):
        for count, groups in (stages[2], (16, wide)):
            piece = piece.reshape(-1, width)
            piece = exchange(jnp.broadcast_to(piece[None], (count,) + piece.shape), groups)
        gram = piece.reshape(8, width, width)
    with jax.named_scope("mixed"):
        mixed = times(panel, gram).astype(jnp.bfloat16)
    with jax.named_scope("mixed_panel"):
        near, far = gather_columns(mixed)
    with jax.named_scope("second"):
        rms_scale = 0.2 * math.sqrt(max(momentum.shape[0] * 96, 3072))
        started = (
            coef_first * momentum.astype(jnp.float32)
            + coef_middle * mixed.astype(jnp.float32)
            + coef_last * times(near, gram[:4])
        )
        total = started + coef_last * times(far, gram[4:])
        return (rms_scale * total).astype(jnp.bfloat16)


def solution(mesh):
    fine = Mesh(mesh.devices.reshape(axis_sizes), axes)
    return jax.shard_map(
        body,
        mesh=fine,
        in_specs=(P(row_axes, col_axes),),
        out_specs=P(row_axes, col_axes),
        check_vma=False,
    )
```
